32 devices in a mesh: dp: 2 (over x), ctx: 4 (over y, core), tensor: 4 (over z).
Axes of the slice: x: 2, y: 2, z: 4, core: 2. Of those that a mesh axis runs over, the one named last changes fastest.
Arguments:
- queries: bfloat16 [1024, 3072], P(('dp', 'ctx'), 'tensor'), parts along dimension 0, may hold values from -6 to 6
- keys: bfloat16 [1024, 512], P(('dp', 'ctx'), 'tensor'), parts along dimension 0, may hold values from -6 to 6
- values: bfloat16 [1024, 512], P(('dp', 'ctx'), 'tensor'), parts along dimension 0, may hold values from -6 to 6
- cache_keys: bfloat16 [1024, 512], P(('dp', 'ctx'), 'tensor'), parts along dimension 0, may hold values from -6 to 6
- cache_values: bfloat16 [1024, 512], P(('dp', 'ctx'), 'tensor'), parts along dimension 0, may hold values from -6 to 6
- residual: bfloat16 [1024, 3072], P(('dp', 'ctx'), 'tensor'), parts along dimension 0, may hold values from -36 to 36
- norm_gain: float32 [3072], replicated, may hold values from 0.1 to 1.9
- w_gate: bfloat16 [3072, 65536], P(None, ('ctx', 'tensor')), may hold values from -0.109375 to 0.109375
- w_up: bfloat16 [3072, 65536], P(None, ('ctx', 'tensor')), may hold values from -0.109375 to 0.109375
- w_down: bfloat16 [65536, 3072], P(('ctx', 'tensor')), may hold values from -0.0625 to 0.0625
- expert_ids: int32 [1024, 2], P(('dp', 'ctx')), parts along dimension 0, may hold values from 0 to 7, all different within a row; in each aligned block of 128 rows (0 to 127, 128 to 255, ...) at most 36 rows name the same one
- gate_weights: float32 [1024, 2], P(('dp', 'ctx')), parts along dimension 0, may hold values from 0.1 to 0.9
Outputs:
- layer_out: bfloat16 [1024, 3072], P(('dp', 'ctx'), 'tensor'), parts along dimension 0
The draws below stay inside these ranges and needn't reach their ends.
There are 2 independent parts, one for each index of `dp`. The reference program is written for one: setup_inputs(seed, part) draws one part's arguments, and reference() takes and returns one part's arrays. A program takes and returns all parts, laid end to end along the dimension named above; an argument that names none is the same for every part. Nothing has to cross between parts.
Inputs may be any that keep to these rules, and one draw needn't show every extreme that they name: `expert_ids`: among the 128 rows of each index of ctx (aligned blocks of rows), no expert is named by more than 36 rows, a bound that some block reaches.
All inputs are finite; a program needn't handle non-finite values.
Results may differ from the reference program's by a relative error of at most 0.012.
Values may be sent and summed in bfloat16 or wider, within the bound.
A program may use at most 192 MiB of HBM per device.

```python
import math
import jax
import jax.numpy as jnp
import numpy as np
from jax import lax

D = 3072
HEADS = 24
KV_HEADS = 4
HEAD_DIM = 128
FF = 8192
EXPERTS = 8
TOP = 2
TOK_DEV = 128
CAP = 36
TOKENS = 512
N_CTX = 4


def draw_queries(key, part):
    drawn_key = jax.random.fold_in(key, 17)
    drawn_draw = jax.random.truncated_normal(drawn_key, -6.0, 6.0, (TOKENS, HEADS * HEAD_DIM), jnp.float32)
    return drawn_draw.astype(jnp.bfloat16)


def draw_keys(key, part):
    drawn_key = jax.random.fold_in(key, 29)
    drawn_draw = jax.random.truncated_normal(drawn_key, -6.0, 6.0, (TOKENS, KV_HEADS * HEAD_DIM), jnp.float32)
    return drawn_draw.astype(jnp.bfloat16)


def draw_residual(key, part):
    row_key, col_key, val_key = jax.random.split(jax.random.fold_in(key, 23), 3)
    row_scale = jnp.exp(jax.random.uniform(row_key, (TOKENS, 1), jnp.float32, math.log(0.3), math.log(3.0)))
    col_scale = jnp.exp(jax.random.uniform(col_key, (1, D), jnp.float32, math.log(0.3), math.log(3.0)))
    drawn_draw = jax.random.truncated_normal(val_key, -4.0, 4.0, (TOKENS, D), jnp.float32)
    return (drawn_draw * row_scale * col_scale).astype(jnp.bfloat16)


def shard_levels(own_key, extent, shards, smallest, high):
    gain = 1.0
    for dim, shards_of in shards:
        heights = jax.random.uniform(jax.random.fold_in(jax.random.fold_in(own_key, 6), dim), (shards_of,), jnp.float32, smallest / len(shards), high / len(shards))
        gain = gain * jnp.repeat(jnp.exp(heights), extent[dim] // shards_of).reshape((-1,) + (1,) * (len(extent) - 1 - dim))
    return gain


def routed_block(rng, own, number, rows, count, top, limit, lean):
    ranking = jax.random.permutation(rng, count)
    packed, common = shares(count, rows * top, limit, lean, True), shares(count, rows * top, limit, lean, False)
    places = jnp.arange(count)

    def named(lengths, offset_by):
        used = int((lengths > 0).sum())
        fixed = max(1, used // 4)
        moved = fixed + (places - fixed + offset_by * (used - fixed)) % max(1, count - fixed)
        return jnp.zeros((count,), jnp.int32).at[ranking[jnp.where(places < fixed, places, moved)]].set(jnp.asarray(lengths, jnp.int32))

    lengths = jnp.where(number % 4 == 0, named(packed, number // 4), named(common, number - number // 4 - 1))
    mixed = jax.random.permutation(jax.random.fold_in(own, 3), count)
    giver, sink = mixed[0:count // 2 * 2:2], mixed[1:count // 2 * 2:2]
    slack = jnp.minimum(lengths[giver] - 1, limit - lengths[sink]) // 2
    slack = jnp.where((giver == ranking[0]) | (sink == ranking[0]) | (lengths[sink] == 0), 0, jnp.maximum(slack, 0))
    moved = jax.random.randint(jax.random.fold_in(own, 4), (count // 2,), 0, 1 << 20) % (slack + 1)
    lengths = lengths.at[giver].add(-moved).at[sink].add(moved)
    items = jnp.searchsorted(jnp.cumsum(lengths), jnp.arange(rows * top), side="right").astype(jnp.int32)
    listing = items.reshape(top, rows).T
    listing = listing[jax.random.permutation(jax.random.fold_in(own, 1), rows)]
    offset_by = jax.random.randint(jax.random.fold_in(own, 2), (rows, 1), 0, top)
    return jnp.take_along_axis(listing, (jnp.arange(top)[None, :] + offset_by) % top, axis=1)


def shares(number_of, total, bound, slope, full):
    weights = [(1 << 20) // math.isqrt(standing ** slope) + 1 for standing in range(1, number_of + 1)]
    largest = bound if full else min(bound, max(-(-total // number_of), total * weights[0] // sum(weights)))
    least = 1 if total - largest >= number_of - 1 else 0
    counts, rest = [largest] + [least] * (number_of - 1), total - largest - least * (number_of - 1)
    while rest > 0:
        candidates = [i for i in range(1, number_of) if counts[i] < largest] or [i for i in range(1, number_of) if counts[i] < bound]
        pool, remaining = sum([weights[i] for i in candidates]), rest
        for i in candidates:
            extra = min(bound - counts[i], max(1, remaining * weights[i] // pool), rest)
            counts[i] = counts[i] + extra
            rest = rest - extra
    return np.array(counts)


def centred(rng, dims, deviation, most, pieces=(), kind=jnp.bfloat16):
    entries = deviation * jax.random.normal(rng, dims, jnp.float32)
    if pieces:
        entries = entries * shard_levels(rng, dims, pieces, -0.22, 0.18)
    return jnp.clip(entries, -most, most).astype(kind)


def setup_inputs(seed: int = 0, part: int = 0) -> dict:
    key_list = jax.random.split(jax.random.key(seed), 13)
    own_keys = jax.random.split(jax.random.fold_in(key_list[12], part), 13)
    queries = draw_queries(jax.random.fold_in(jax.random.fold_in(key_list[12], part), 71), part)
    keys = draw_keys(jax.random.fold_in(jax.random.fold_in(key_list[12], part), 71), part)
    values = centred(own_keys[2], (TOKENS, KV_HEADS * HEAD_DIM), 1.0, 6.0, ((0, 4), (1, 4)))
    cache_keys = centred(own_keys[3], (TOKENS, KV_HEADS * HEAD_DIM), 1.0, 6.0, ((0, 4), (1, 4)))
    cache_values = centred(own_keys[4], (TOKENS, KV_HEADS * HEAD_DIM), 1.0, 6.0, ((0, 4), (1, 4)))
    residual = draw_residual(jax.random.fold_in(jax.random.fold_in(key_list[12], part), 71), part)
    norm_gain = jnp.clip(1.0 + 0.18 * jax.random.normal(key_list[6], (D,), jnp.float32), 0.1, 1.9)
    w_gate = centred(key_list[7], (D, EXPERTS * FF), D ** -0.5, 0.109375, ((1, 16),))
    w_up = centred(key_list[8], (D, EXPERTS * FF), D ** -0.5, 0.109375, ((1, 16),))
    w_down = centred(key_list[9], (EXPERTS * FF, D), FF ** -0.5, 0.0625, ((0, 16),))
    expert_ids_keys = jax.random.split(jax.random.fold_in(own_keys[10], 1), TOKENS // TOK_DEV)
    expert_ids_turns = jax.random.permutation(jax.random.fold_in(own_keys[10], 3), TOKENS // TOK_DEV)
    expert_ids = jax.vmap(lambda own, number: routed_block(jax.random.fold_in(own_keys[10], 2), own, number, TOK_DEV, EXPERTS, TOP, CAP, 1))(expert_ids_keys, expert_ids_turns).reshape((TOKENS, TOP))
    gate_weights = jnp.clip(0.1 + 0.79999997 * jax.random.uniform(own_keys[11], (TOKENS, TOP), jnp.float32) ** shard_levels(own_keys[11], (TOKENS, TOP), ((0, 4),), -0.2, 0.2), 0.1, 0.9)
    return dict(queries=queries, keys=keys, values=values, cache_keys=cache_keys, cache_values=cache_values, residual=residual, norm_gain=norm_gain, w_gate=w_gate, w_up=w_up, w_down=w_down, expert_ids=expert_ids, gate_weights=gate_weights)


eps = 1e-05
neg_big = -1e+30

def reference(queries, keys, values, cache_keys, cache_values, residual, norm_gain, w_gate, w_up, w_down, expert_ids, gate_weights):
    window = TOKENS
    group_size = HEADS // KV_HEADS
    score_scale = 1.0 / math.sqrt(HEAD_DIM)
    all_keys = jnp.concatenate((cache_keys, keys), axis=0)
    all_values = jnp.concatenate((cache_values, values), axis=0)
    offsets = jnp.arange(TOKENS, dtype=jnp.int32)
    key_pos = jnp.concatenate((offsets - window, offsets))
    allowed = (key_pos[None, :] <= offsets[:, None]) & (key_pos[None, :] > offsets[:, None] - window)

    def one_head(head_index):
        kv_head = head_index // group_size
        head_query = lax.dynamic_slice_in_dim(queries, head_index * HEAD_DIM, HEAD_DIM, 1)
        head_keys = lax.dynamic_slice_in_dim(all_keys, kv_head * HEAD_DIM, HEAD_DIM, 1)
        head_values = lax.dynamic_slice_in_dim(all_values, kv_head * HEAD_DIM, HEAD_DIM, 1)
        scores = jnp.dot(head_query, head_keys.T, preferred_element_type=jnp.float32) * score_scale
        scores = jnp.where(allowed, scores, neg_big)
        row_max = lax.optimization_barrier(jnp.max(scores, axis=1, keepdims=True))
        weights = jnp.where(allowed, jnp.exp(scores - row_max), 0.0)
        row_total = lax.optimization_barrier(jnp.sum(weights, axis=1, keepdims=True))
        summed = jnp.dot(weights.astype(jnp.bfloat16), head_values, preferred_element_type=jnp.float32)
        return summed / row_total
    heads_out = lax.map(one_head, jnp.arange(HEADS, dtype=jnp.int32))
    attended = jnp.transpose(heads_out, (1, 0, 2)).reshape(TOKENS, HEADS * HEAD_DIM)
    hidden_state = (residual.astype(jnp.float32) + attended).astype(jnp.bfloat16)
    widened = hidden_state.astype(jnp.float32)
    inverse = lax.rsqrt(lax.optimization_barrier(jnp.mean(widened * widened, axis=1, keepdims=True)) + eps)
    normed = (widened * inverse * norm_gain).astype(jnp.bfloat16)
    row_limit = N_CTX * CAP

    def one_expert(mixture, expert):
        chosen = expert_ids == expert
        weight = lax.optimization_barrier(jnp.sum(jnp.where(chosen, gate_weights, 0.0), axis=1))
        routed = jnp.any(chosen, axis=1)
        row_ids = jnp.nonzero(routed, size=row_limit, fill_value=0)[0].astype(jnp.int32)
        filled = jnp.arange(row_limit, dtype=jnp.int32) < jnp.sum(routed.astype(jnp.int32))
        picked = jnp.take(normed, row_ids, axis=0)
        gate_proj = jnp.dot(picked, lax.dynamic_slice_in_dim(w_gate, expert * FF, FF, 1), preferred_element_type=jnp.float32)
        up_proj = jnp.dot(picked, lax.dynamic_slice_in_dim(w_up, expert * FF, FF, 1), preferred_element_type=jnp.float32)
        activated = (jax.nn.silu(gate_proj) * up_proj).astype(jnp.bfloat16)
        outcome = jnp.dot(activated, lax.dynamic_slice_in_dim(w_down, expert * FF, FF, 0), preferred_element_type=jnp.float32)
        scaled = outcome * jnp.where(filled, jnp.take(weight, row_ids), 0.0)[:, None]
        return (mixture.at[row_ids].add(scaled), None)
    mixture, _ = lax.scan(one_expert, jnp.zeros((TOKENS, D), jnp.float32), jnp.arange(EXPERTS, dtype=jnp.int32))
    return (widened + mixture).astype(jnp.bfloat16)
```

```python
import math

import jax
import jax.numpy as jnp
from jax import lax
from jax.experimental import pallas as pl
from jax.experimental.pallas import tpu as pltpu
from jax.sharding import PartitionSpec as P

HEADS = 24
KV_HEADS = 4
HEAD_DIM = 128
EXPERTS = 8
TOP = 2
CAP = 36


eps = 1e-05
neg_big = -1e30


def attend_block(
    carried, query_heads, key_block, value_block, key_pos, query_pos, window, score_scale
):
    run_max, run_sum, accumulated = carried
    scores = (
        jnp.einsum("qkgd,tkd->kgqt", query_heads, key_block, preferred_element_type=jnp.float32)
        * score_scale
    )
    allowed = (key_pos[None, :] <= query_pos[:, None]) & (
        key_pos[None, :] > query_pos[:, None] - window
    )
    scores = jnp.where(allowed[None, None], scores, neg_big)
    new_max = jnp.maximum(run_max, jnp.max(scores, axis=-1))
    weights = jnp.where(allowed[None, None], jnp.exp(scores - new_max[..., None]), 0.0)
    run_sum = jnp.sum(weights, axis=-1)
    update = jnp.einsum(
        "kgqt,tkd->kgqd",
        weights.astype(jnp.bfloat16),
        value_block,
        preferred_element_type=jnp.float32,
    )
    accumulated = update
    return (new_max, run_sum, accumulated)


def expert_block(full_rows, norm_gain, w_gate, w_up, w_down):
    widened = full_rows.astype(jnp.float32)
    inverse = lax.rsqrt(jnp.mean(widened * widened, axis=-1, keepdims=True) + eps)
    normed = (widened * inverse * norm_gain).astype(jnp.bfloat16)
    gate_proj = jnp.dot(normed, w_gate, preferred_element_type=jnp.float32)
    up_proj = jnp.dot(normed, w_up, preferred_element_type=jnp.float32)
    activated = (jax.nn.silu(gate_proj) * up_proj).astype(jnp.bfloat16)
    return jnp.dot(activated, w_down, preferred_element_type=jnp.float32)


def route_tables(expert_ids, gate_weights):
    tok_rows = expert_ids.shape[0]
    flat_ids = expert_ids.reshape(-1)
    member = (flat_ids[:, None] == jnp.arange(EXPERTS, dtype=jnp.int32)[None, :]).astype(jnp.int32)
    earlier = jnp.cumsum(member, axis=0) - member
    rank_in = jnp.sum(earlier * member, axis=1)
    slot_of = flat_ids * CAP + rank_in
    picks = (jnp.arange(EXPERTS * CAP, dtype=jnp.int32)[:, None] == slot_of[None, :]).astype(
        jnp.float32
    )
    select = jnp.sum(picks.reshape(EXPERTS * CAP, tok_rows, TOP), axis=2).astype(jnp.bfloat16)
    weighing = jnp.sum(
        (picks * gate_weights.reshape(-1)[None, :]).reshape(EXPERTS * CAP, tok_rows, TOP), axis=2
    )
    return (select, weighing)


def per_device(
    queries,
    keys,
    values,
    cache_keys,
    cache_values,
    residual,
    norm_gain,
    w_gate,
    w_up,
    w_down,
    expert_ids,
    gate_weights,
):
    tok_rows = queries.shape[0]
    n_ctx = lax.axis_size("ctx")
    n_tensor = lax.axis_size("tensor")
    window = tok_rows * n_ctx
    kv_local = keys.shape[1] // HEAD_DIM
    group_size = HEADS // KV_HEADS
    score_scale = 1.0 / math.sqrt(HEAD_DIM)
    query_heads = queries.reshape(tok_rows, kv_local, group_size, HEAD_DIM)
    my_index = lax.axis_index("ctx")
    query_pos = my_index * tok_rows + jnp.arange(tok_rows, dtype=jnp.int32)
    initial = (
        jnp.full((kv_local, group_size, tok_rows), neg_big, jnp.float32),
        jnp.zeros((kv_local, group_size, tok_rows), jnp.float32),
        jnp.zeros((kv_local, group_size, tok_rows, HEAD_DIM), jnp.float32),
    )
    stacked = jnp.stack((cache_keys, cache_values, keys, values))
    shard_piece = lax.all_gather(stacked, "ctx", axis=1, tiled=True)
    span_rows = shard_piece.shape[1]
    offsets = jnp.arange(span_rows, dtype=jnp.int32)
    key_block = jnp.concatenate((shard_piece[0], shard_piece[2]), axis=0).reshape(
        2 * span_rows, kv_local, HEAD_DIM
    )
    value_block = jnp.concatenate((shard_piece[1], shard_piece[3]), axis=0).reshape(
        2 * span_rows, kv_local, HEAD_DIM
    )
    key_pos = jnp.concatenate((offsets - window, offsets))
    run_max, run_sum, accumulated = attend_block(
        initial, query_heads, key_block, value_block, key_pos, query_pos, window, score_scale
    )
    attended = (
        (accumulated / run_sum[..., None])
        .transpose(2, 0, 1, 3)
        .reshape(tok_rows, kv_local * group_size * HEAD_DIM)
    )
    hidden_state = (residual.astype(jnp.float32) + attended).astype(jnp.bfloat16)
    select, weighing = route_tables(expert_ids, gate_weights)
    quarter = hidden_state.shape[1]
    buffer = (
        jnp.dot(select, hidden_state, preferred_element_type=jnp.float32)
        .astype(jnp.bfloat16)
        .reshape(EXPERTS, CAP, quarter)
    )
    per_expert = n_ctx * n_tensor // EXPERTS
    outgoing = jnp.repeat(buffer, per_expert, axis=0)
    arrived = lax.all_to_all(outgoing, ("ctx", "tensor"), split_axis=0, concat_axis=2, tiled=True)
    item_count = arrived.shape[1]
    full_rows = arrived.reshape(item_count * n_ctx, n_tensor * quarter)
    partial_value = expert_block(full_rows, norm_gain, w_gate, w_up, w_down)
    gathered_parts = lax.all_to_all(
        partial_value.reshape(item_count, n_ctx * n_tensor, quarter).astype(jnp.bfloat16),
        ("ctx", "tensor"),
        split_axis=1,
        concat_axis=1,
        tiled=True,
    ).astype(jnp.float32)
    expert_out = (
        jnp.sum(gathered_parts.reshape(CAP, EXPERTS, per_expert, quarter), axis=2)
        .transpose(1, 0, 2)
        .reshape(EXPERTS * CAP, quarter)
    )
    mixture = lax.dot_general(
        weighing,
        expert_out,
        (((0,), (0,)), ((), ())),
        precision=lax.Precision.HIGHEST,
        preferred_element_type=jnp.float32,
    )
    return (hidden_state.astype(jnp.float32) + mixture).astype(jnp.bfloat16)


MAIN = 32
TAIL = 16
LANES = 256
BLOCK = 512
GATE_SLOTS = 5
DOWN_SLOTS = 3
MESH = pl.DeviceIdType.MESH
f32 = jnp.float32
bf16 = jnp.bfloat16


def iota(shape, dim):
    return lax.broadcasted_iota(jnp.int32, shape, dim)


def nt_dot(a, b):
    return lax.dot_general(a, b, (((1,), (1,)), ((), ())), preferred_element_type=f32)


def layer_kernel(
    n_ctx,
    n_tensor,
    q_ref,
    k_ref,
    v_ref,
    ck_ref,
    cv_ref,
    res_ref,
    gain_ref,
    ids_ref,
    gw_ref,
    wg_hbm,
    wu_hbm,
    wd_hbm,
    o_ref,
    wg_buf,
    wu_buf,
    wd_buf,
    kv_own,
    kv_buf,
    hid,
    msg,
    got,
    xs,
    act,
    back,
    landed,
    pick_main,
    pick_tail,
    gate_sem,
    up_sem,
    down_sem,
    kv_send,
    kv_recv,
    out_send,
    out_recv,
    back_send,
    back_recv,
):
    c = lax.axis_index("ctx")
    z = lax.axis_index("tensor")
    me = c * n_tensor + z
    rows, quarter = res_ref.shape
    groups = quarter // LANES
    hidden = wd_hbm.shape[0]
    n_blocks = hidden // BLOCK
    per_expert = n_ctx * n_tensor // EXPERTS
    n_dev = n_ctx * n_tensor

    z_order = (
        (2, lax.rem(z + 2, 4)),
        (3, 3 - z),
        (1, z + 1 - 2 * lax.rem(z, 2)),
        (0, z),
    )

    def ctx_at(dc):
        return lax.rem(c + dc, n_ctx)

    barrier = pltpu.get_barrier_semaphore()
    for jz, zp in z_order:
        for dc in range(n_ctx):
            if jz or dc:
                pl.semaphore_signal(
                    barrier,
                    inc=1,
                    device_id={"ctx": ctx_at(dc), "tensor": zp},
                    device_id_type=MESH,
                )
    kv_own[0, 0] = ck_ref[...]
    kv_own[0, 1] = cv_ref[...]
    kv_own[1, 0] = k_ref[...]
    kv_own[1, 1] = v_ref[...]
    pl.semaphore_wait(barrier, n_dev - 1)

    kv_copies = []
    for dc in range(1, n_ctx):
        copy = pltpu.make_async_remote_copy(
            src_ref=kv_own.at[1 - (c + dc) // n_ctx],
            dst_ref=kv_buf.at[c],
            send_sem=kv_send.at[dc],
            recv_sem=kv_recv.at[c],
            device_id={"ctx": ctx_at(dc), "tensor": z},
            device_id_type=MESH,
        )
        copy.start()
        kv_copies.append(copy)

    def gate_copy(b):
        slot = lax.rem(b, GATE_SLOTS)
        cols = pl.ds(pl.multiple_of(b * BLOCK, BLOCK), BLOCK)
        return (
            pltpu.make_async_copy(wg_hbm.at[:, cols], wg_buf.at[slot], gate_sem.at[slot]),
            pltpu.make_async_copy(wu_hbm.at[:, cols], wu_buf.at[slot], up_sem.at[slot]),
        )

    def down_copy(step):
        zp = z_order[step][1]
        slot = step % DOWN_SLOTS
        cols = pl.ds(pl.multiple_of(zp * quarter, quarter), quarter)
        return pltpu.make_async_copy(wd_hbm.at[:, cols], wd_buf.at[slot], down_sem.at[slot])

    for b in range(GATE_SLOTS):
        for copy in gate_copy(jnp.int32(b)):
            copy.start()
    for step in range(DOWN_SLOTS):
        down_copy(step).start()

    ids = ids_ref[...]
    id_k = (ids[:, 0:1], ids[:, 1:2])
    lane = iota((rows, 128), 1)
    member = ((lane == id_k[0]) | (lane == id_k[1])).astype(f32).astype(bf16)
    earlier = (iota((rows, rows), 0) > iota((rows, rows), 1)).astype(f32).astype(bf16)
    count = jnp.dot(earlier, member, preferred_element_type=f32)
    rank_k = tuple(
        jnp.sum(jnp.where(lane == e, count, 0.0), axis=1, keepdims=True).astype(jnp.int32)
        for e in id_k
    )

    l_main = iota((rows, EXPERTS * MAIN), 1)
    s_main = jnp.zeros((rows, EXPERTS * MAIN), f32)
    l_tail = iota((rows, EXPERTS * TAIL), 1)
    s_tail = jnp.zeros((rows, EXPERTS * TAIL), f32)
    for k in range(TOP):
        s_main += (
            (id_k[k] == l_main // MAIN) & (rank_k[k] == l_main % MAIN)
        ).astype(f32)
        s_tail += (
            (id_k[k] == l_tail // TAIL) & (rank_k[k] == MAIN + l_tail % 4)
        ).astype(f32)
    s_main = s_main.T.astype(bf16)
    s_tails = [
        jnp.where(l_tail % TAIL // 4 == g, s_tail, 0.0).T.astype(bf16) for g in range(groups)
    ]
    p_main = iota((rows, n_dev * MAIN), 1)
    p_tail = iota((rows, n_dev * TAIL), 1)
    for k in range(TOP):
        pick_main[k] = (
            ((id_k[k] == p_main // (MAIN * per_expert)) & (rank_k[k] == p_main % MAIN))
            .astype(f32)
            .astype(bf16)
        )
        for g in range(groups):
            pick_tail[k, g] = (
                (
                    (id_k[k] == p_tail // (TAIL * per_expert))
                    & (rank_k[k] == MAIN + p_tail % 4)
                    & (p_tail % TAIL // 4 == g)
                )
                .astype(f32)
                .astype(bf16)
            )

    for dc in range(1, n_ctx):
        peer = ctx_at(dc)
        pltpu.make_async_remote_copy(
            src_ref=kv_own.at[0],
            dst_ref=kv_buf.at[peer],
            send_sem=kv_send.at[0],
            recv_sem=kv_recv.at[peer],
            device_id={"ctx": peer, "tensor": z},
            device_id_type=MESH,
        ).wait_recv()
    key_rest = jnp.concatenate([kv_buf[ctx_at(dc), 0] for dc in range(1, n_ctx)], axis=0)
    value_rest = jnp.concatenate([kv_buf[ctx_at(dc), 1] for dc in range(1, n_ctx)], axis=0)
    seen = iota((rows, rows), 1) <= iota((rows, rows), 0)
    scale = 1.0 / math.sqrt(HEAD_DIM)
    for h in range(quarter // HEAD_DIM):
        cols = slice(h * HEAD_DIM, (h + 1) * HEAD_DIM)
        head = q_ref[:, cols]
        s_rest = nt_dot(head, key_rest) * scale
        s_own = jnp.where(seen, nt_dot(head, k_ref[...]), nt_dot(head, ck_ref[...])) * scale
        top = jnp.maximum(
            jnp.max(s_rest, axis=1, keepdims=True), jnp.max(s_own, axis=1, keepdims=True)
        )
        w_rest = jnp.exp(s_rest - top)
        w_own = jnp.exp(s_own - top)
        total = jnp.sum(w_rest, axis=1, keepdims=True) + jnp.sum(w_own, axis=1, keepdims=True)
        summed = jnp.dot(w_rest.astype(bf16), value_rest, preferred_element_type=f32)
        summed += jnp.dot(
            jnp.where(seen, w_own, 0.0).astype(bf16), v_ref[...], preferred_element_type=f32
        )
        summed += jnp.dot(
            jnp.where(seen, 0.0, w_own).astype(bf16), cv_ref[...], preferred_element_type=f32
        )
        hid[:, cols] = (res_ref[:, cols].astype(f32) + summed / total).astype(bf16)

    tails = jnp.zeros((EXPERTS * TAIL, LANES), f32)
    for g in range(groups):
        part = hid[:, g * LANES : (g + 1) * LANES]
        chosen = jnp.dot(s_main, part, preferred_element_type=f32).astype(bf16)
        msg[:, g * MAIN : (g + 1) * MAIN, :] = chosen.reshape(EXPERTS, MAIN, LANES)
        tails += jnp.dot(s_tails[g], part, preferred_element_type=f32)
    msg[:, groups * MAIN :, :] = tails.astype(bf16).reshape(EXPERTS, TAIL, LANES)
    out_copies = []
    for jz, zp in z_order:
        for dc in range(n_ctx):
            cp = ctx_at(dc)
            to = (cp * n_tensor + zp) // per_expert
            if jz or dc:
                copy = pltpu.make_async_remote_copy(
                    src_ref=msg.at[to],
                    dst_ref=got.at[c, z],
                    send_sem=out_send.at[jz * n_ctx + dc],
                    recv_sem=out_recv.at[me],
                    device_id={"ctx": cp, "tensor": zp},
                    device_id_type=MESH,
                )
                copy.start()
                out_copies.append(copy)
            else:
                got[c, z] = msg[to]
    for jz, zp in z_order[::-1]:
        for dc in range(n_ctx):
            if jz or dc:
                cp = ctx_at(dc)
                pltpu.make_async_remote_copy(
                    src_ref=msg.at[0],
                    dst_ref=got.at[cp, zp],
                    send_sem=out_send.at[0],
                    recv_sem=out_recv.at[cp * n_tensor + zp],
                    device_id={"ctx": cp, "tensor": zp},
                    device_id_type=MESH,
                ).wait_recv()

    def normed(full):
        wide = full.astype(f32)
        inverse = lax.rsqrt(jnp.mean(wide * wide, axis=1, keepdims=True) + eps)
        return (wide * inverse * gain_ref[...]).astype(bf16)

    for cp in range(n_ctx):
        full = jnp.concatenate(
            [
                got[cp, q, g * MAIN : (g + 1) * MAIN, :]
                for q in range(n_tensor)
                for g in range(groups)
            ],
            axis=1,
        )
        xs[cp * MAIN : (cp + 1) * MAIN, :] = normed(full)
    fold_r = iota((n_ctx * 4, n_ctx * TAIL), 0)
    fold_c = iota((n_ctx * 4, n_ctx * TAIL), 1)
    fold = [
        (
            (fold_r // 4 == fold_c // TAIL)
            & (fold_r % 4 == fold_c % 4)
            & (fold_c % TAIL // 4 == g)
        )
        .astype(f32)
        .astype(bf16)
        for g in range(groups)
    ]
    ends = []
    for q in range(n_tensor):
        folded = got[:, q, groups * MAIN :, :].reshape(n_ctx * TAIL, LANES)
        for g in range(groups):
            ends.append(jnp.dot(fold[g], folded, preferred_element_type=f32))
    xs[n_ctx * MAIN :, :] = normed(jnp.concatenate(ends, axis=1))

    def gate_block(b, carry):
        slot = lax.rem(b, GATE_SLOTS)
        for copy in gate_copy(b):
            copy.wait()
        gate = jnp.dot(xs[...], wg_buf[slot], preferred_element_type=f32)
        up = jnp.dot(xs[...], wu_buf[slot], preferred_element_type=f32)
        low = (gate / (1.0 + jnp.exp(-gate)) * up).astype(bf16)
        act[:, pl.ds(pl.multiple_of(b * BLOCK, BLOCK), BLOCK)] = low

        @pl.when(b + GATE_SLOTS < n_blocks)
        def _():
            for copy in gate_copy(b + GATE_SLOTS):
                copy.start()

        return carry

    lax.fori_loop(0, n_blocks, gate_block, 0)

    fold_r = iota((n_ctx * TAIL, n_ctx * 4), 0)
    fold_c = iota((n_ctx * TAIL, n_ctx * 4), 1)
    back_copies = []
    for step, (jz, zp) in enumerate(z_order):
        down_copy(step).wait()
        part = jnp.dot(
            act[...], wd_buf[step % DOWN_SLOTS], preferred_element_type=f32
        ).astype(bf16)
        if step + DOWN_SLOTS < n_tensor:
            down_copy(step + DOWN_SLOTS).start()
        tails = jnp.zeros((n_ctx * TAIL, LANES), f32)
        for g in range(groups):
            cols = slice(g * LANES, (g + 1) * LANES)
            back[jz, :, g * MAIN : (g + 1) * MAIN, :] = part[: n_ctx * MAIN, cols].reshape(
                n_ctx, MAIN, LANES
            )
            unfold = (
                (
                    (fold_c // 4 == fold_r // TAIL)
                    & (fold_c % 4 == fold_r % 4)
                    & (fold_r % TAIL // 4 == g)
                )
                .astype(f32)
                .astype(bf16)
            )
            tails += jnp.dot(unfold, part[n_ctx * MAIN :, cols], preferred_element_type=f32)
        back[jz, :, groups * MAIN :, :] = tails.astype(bf16).reshape(n_ctx, TAIL, LANES)
        for dc in range(n_ctx):
            cp = ctx_at(dc)
            if jz or dc:
                copy = pltpu.make_async_remote_copy(
                    src_ref=back.at[jz, cp],
                    dst_ref=landed.at[me],
                    send_sem=back_send.at[jz * n_ctx + dc],
                    recv_sem=back_recv.at[me],
                    device_id={"ctx": cp, "tensor": zp},
                    device_id_type=MESH,
                )
                copy.start()
                back_copies.append(copy)
            else:
                landed[me] = back[jz, cp]
    for jz, zp in z_order[::-1]:
        for dc in range(n_ctx):
            if jz or dc:
                cp = ctx_at(dc)
                peer = cp * n_tensor + zp
                pltpu.make_async_remote_copy(
                    src_ref=back.at[0, 0],
                    dst_ref=landed.at[peer],
                    send_sem=back_send.at[0],
                    recv_sem=back_recv.at[peer],
                    device_id={"ctx": cp, "tensor": zp},
                    device_id_type=MESH,
                ).wait_recv()

    ends = landed[:, groups * MAIN :, :].reshape(n_dev * TAIL, LANES)
    for g in range(groups):
        cols = slice(g * LANES, (g + 1) * LANES)
        body = landed[:, g * MAIN : (g + 1) * MAIN, :].reshape(n_dev * MAIN, LANES)
        sums = hid[:, cols].astype(f32)
        for k in range(TOP):
            found = jnp.dot(pick_main[k], body, preferred_element_type=f32)
            found += jnp.dot(pick_tail[k, g], ends, preferred_element_type=f32)
            sums += gw_ref[:, k : k + 1] * found
        o_ref[:, cols] = sums.astype(bf16)
    for copy in kv_copies + out_copies + back_copies:
        copy.wait_send()


def fused(
    queries,
    keys,
    values,
    cache_keys,
    cache_values,
    residual,
    norm_gain,
    w_gate,
    w_up,
    w_down,
    expert_ids,
    gate_weights,
):
    n_ctx = lax.axis_size("ctx")
    n_tensor = lax.axis_size("tensor")
    rows, quarter = residual.shape
    width = w_gate.shape[0]
    hidden = w_gate.shape[1]
    n_dev = n_ctx * n_tensor
    length = quarter // LANES * MAIN + TAIL
    items = n_ctx * CAP
    vmem = pl.BlockSpec(memory_space=pltpu.VMEM)
    hbm = pl.BlockSpec(memory_space=pl.ANY)
    dma = pltpu.SemaphoreType.DMA

    def kernel(*refs):
        layer_kernel(n_ctx, n_tensor, *refs)

    return pl.pallas_call(
        kernel,
        out_shape=jax.ShapeDtypeStruct(residual.shape, bf16),
        in_specs=[vmem] * 9 + [hbm] * 3,
        out_specs=vmem,
        scratch_shapes=[
            pltpu.VMEM((GATE_SLOTS, width, BLOCK), bf16),
            pltpu.VMEM((GATE_SLOTS, width, BLOCK), bf16),
            pltpu.VMEM((DOWN_SLOTS, hidden, quarter), bf16),
            pltpu.VMEM((2, 2, rows, HEAD_DIM), bf16),
            pltpu.VMEM((n_ctx, 2, rows, HEAD_DIM), bf16),
            pltpu.VMEM((rows, quarter), bf16),
            pltpu.VMEM((EXPERTS, length, LANES), bf16),
            pltpu.VMEM((n_ctx, n_tensor, length, LANES), bf16),
            pltpu.VMEM((items, width), bf16),
            pltpu.VMEM((items, hidden), bf16),
            pltpu.VMEM((n_tensor, n_ctx, length, LANES), bf16),
            pltpu.VMEM((n_dev, length, LANES), bf16),
            pltpu.VMEM((TOP, rows, n_dev * MAIN), bf16),
            pltpu.VMEM((TOP, quarter // LANES, rows, n_dev * TAIL), bf16),
            dma((GATE_SLOTS,)),
            dma((GATE_SLOTS,)),
            dma((DOWN_SLOTS,)),
            dma((n_ctx,)),
            dma((n_ctx,)),
            dma((n_dev,)),
            dma((n_dev,)),
            dma((n_dev,)),
            dma((n_dev,)),
        ],
        compiler_params=pltpu.CompilerParams(
            collective_id=0, has_side_effects=True, vmem_limit_bytes=60 * 1024 * 1024
        ),
        cost_estimate=pl.CostEstimate(
            flops=6 * items * width * hidden,
            bytes_accessed=6 * width * hidden,
            transcendentals=items * hidden,
        ),
    )(
        queries,
        keys,
        values,
        cache_keys,
        cache_values,
        residual,
        norm_gain.reshape(1, width),
        expert_ids,
        gate_weights,
        w_gate,
        w_up,
        w_down,
    )


def solution(mesh):
    in_specs = (
        P(("dp", "ctx"), "tensor"),
        P(("dp", "ctx"), "tensor"),
        P(("dp", "ctx"), "tensor"),
        P(("dp", "ctx"), "tensor"),
        P(("dp", "ctx"), "tensor"),
        P(("dp", "ctx"), "tensor"),
        P(),
        P(None, ("ctx", "tensor")),
        P(None, ("ctx", "tensor")),
        P(("ctx", "tensor"), None),
        P(("dp", "ctx"), None),
        P(("dp", "ctx"), None),
    )
    out_specs = P(("dp", "ctx"), "tensor")
    fits = mesh.shape["ctx"] == 4 and mesh.shape["tensor"] == 4
    return jax.shard_map(
        fused if fits else per_device, mesh=mesh, in_specs=in_specs, out_specs=out_specs, check_vma=False
    )
```

```python
import math

import jax
import jax.numpy as jnp
from jax import lax
from jax.experimental import pallas as pl
from jax.experimental.pallas import tpu as pltpu
from jax.sharding import PartitionSpec as P

HEADS = 24
KV_HEADS = 4
HEAD_DIM = 128
EXPERTS = 8
TOP = 2
CAP = 36


eps = 1e-05
neg_big = -1e30


def attend_block(
    carried, query_heads, key_block, value_block, key_pos, query_pos, window, score_scale
):
    run_max, run_sum, accumulated = carried
    scores = (
        jnp.einsum("qkgd,tkd->kgqt", query_heads, key_block, preferred_element_type=jnp.float32)
        * score_scale
    )
    allowed = (key_pos[None, :] <= query_pos[:, None]) & (
        key_pos[None, :] > query_pos[:, None] - window
    )
    scores = jnp.where(allowed[None, None], scores, neg_big)
    new_max = jnp.maximum(run_max, jnp.max(scores, axis=-1))
    weights = jnp.where(allowed[None, None], jnp.exp(scores - new_max[..., None]), 0.0)
    run_sum = jnp.sum(weights, axis=-1)
    update = jnp.einsum(
        "kgqt,tkd->kgqd",
        weights.astype(jnp.bfloat16),
        value_block,
        preferred_element_type=jnp.float32,
    )
    accumulated = update
    return (new_max, run_sum, accumulated)


def expert_block(full_rows, norm_gain, w_gate, w_up, w_down):
    widened = full_rows.astype(jnp.float32)
    inverse = lax.rsqrt(jnp.mean(widened * widened, axis=-1, keepdims=True) + eps)
    normed = (widened * inverse * norm_gain).astype(jnp.bfloat16)
    gate_proj = jnp.dot(normed, w_gate, preferred_element_type=jnp.float32)
    up_proj = jnp.dot(normed, w_up, preferred_element_type=jnp.float32)
    activated = (jax.nn.silu(gate_proj) * up_proj).astype(jnp.bfloat16)
    return jnp.dot(activated, w_down, preferred_element_type=jnp.float32)


def route_tables(expert_ids, gate_weights):
    tok_rows = expert_ids.shape[0]
    flat_ids = expert_ids.reshape(-1)
    member = (flat_ids[:, None] == jnp.arange(EXPERTS, dtype=jnp.int32)[None, :]).astype(jnp.int32)
    earlier = jnp.cumsum(member, axis=0) - member
    rank_in = jnp.sum(earlier * member, axis=1)
    slot_of = flat_ids * CAP + rank_in
    picks = (jnp.arange(EXPERTS * CAP, dtype=jnp.int32)[:, None] == slot_of[None, :]).astype(
        jnp.float32
    )
    select = jnp.sum(picks.reshape(EXPERTS * CAP, tok_rows, TOP), axis=2).astype(jnp.bfloat16)
    weighing = jnp.sum(
        (picks * gate_weights.reshape(-1)[None, :]).reshape(EXPERTS * CAP, tok_rows, TOP), axis=2
    )
    return (select, weighing)


def per_device(
    queries,
    keys,
    values,
    cache_keys,
    cache_values,
    residual,
    norm_gain,
    w_gate,
    w_up,
    w_down,
    expert_ids,
    gate_weights,
):
    tok_rows = queries.shape[0]
    n_ctx = lax.axis_size("ctx")
    n_tensor = lax.axis_size("tensor")
    window = tok_rows * n_ctx
    kv_local = keys.shape[1] // HEAD_DIM
    group_size = HEADS // KV_HEADS
    score_scale = 1.0 / math.sqrt(HEAD_DIM)
    query_heads = queries.reshape(tok_rows, kv_local, group_size, HEAD_DIM)
    my_index = lax.axis_index("ctx")
    query_pos = my_index * tok_rows + jnp.arange(tok_rows, dtype=jnp.int32)
    initial = (
        jnp.full((kv_local, group_size, tok_rows), neg_big, jnp.float32),
        jnp.zeros((kv_local, group_size, tok_rows), jnp.float32),
        jnp.zeros((kv_local, group_size, tok_rows, HEAD_DIM), jnp.float32),
    )
    stacked = jnp.stack((cache_keys, cache_values, keys, values))
    shard_piece = lax.all_gather(stacked, "ctx", axis=1, tiled=True)
    span_rows = shard_piece.shape[1]
    offsets = jnp.arange(span_rows, dtype=jnp.int32)
    key_block = jnp.concatenate((shard_piece[0], shard_piece[2]), axis=0).reshape(
        2 * span_rows, kv_local, HEAD_DIM
    )
    value_block = jnp.concatenate((shard_piece[1], shard_piece[3]), axis=0).reshape(
        2 * span_rows, kv_local, HEAD_DIM
    )
    key_pos = jnp.concatenate((offsets - window, offsets))
    run_max, run_sum, accumulated = attend_block(
        initial, query_heads, key_block, value_block, key_pos, query_pos, window, score_scale
    )
    attended = (
        (accumulated / run_sum[..., None])
        .transpose(2, 0, 1, 3)
        .reshape(tok_rows, kv_local * group_size * HEAD_DIM)
    )
    hidden_state = (residual.astype(jnp.float32) + attended).astype(jnp.bfloat16)
    select, weighing = route_tables(expert_ids, gate_weights)
    quarter = hidden_state.shape[1]
    buffer = (
        jnp.dot(select, hidden_state, preferred_element_type=jnp.float32)
        .astype(jnp.bfloat16)
        .reshape(EXPERTS, CAP, quarter)
    )
    per_expert = n_ctx * n_tensor // EXPERTS
    outgoing = jnp.repeat(buffer, per_expert, axis=0)
    arrived = lax.all_to_all(outgoing, ("ctx", "tensor"), split_axis=0, concat_axis=2, tiled=True)
    item_count = arrived.shape[1]
    full_rows = arrived.reshape(item_count * n_ctx, n_tensor * quarter)
    partial_value = expert_block(full_rows, norm_gain, w_gate, w_up, w_down)
    gathered_parts = lax.all_to_all(
        partial_value.reshape(item_count, n_ctx * n_tensor, quarter).astype(jnp.bfloat16),
        ("ctx", "tensor"),
        split_axis=1,
        concat_axis=1,
        tiled=True,
    ).astype(jnp.float32)
    expert_out = (
        jnp.sum(gathered_parts.reshape(CAP, EXPERTS, per_expert, quarter), axis=2)
        .transpose(1, 0, 2)
        .reshape(EXPERTS * CAP, quarter)
    )
    mixture = lax.dot_general(
        weighing,
        expert_out,
        (((0,), (0,)), ((), ())),
        precision=lax.Precision.HIGHEST,
        preferred_element_type=jnp.float32,
    )
    return (hidden_state.astype(jnp.float32) + mixture).astype(jnp.bfloat16)


MAIN = 32
TAIL = 16
LANES = 256
BLOCK = 512
GATE_SLOTS = 3
DOWN_SLOTS = 2
MESH = pl.DeviceIdType.MESH
f32 = jnp.float32
bf16 = jnp.bfloat16


def iota(shape, dim):
    return lax.broadcasted_iota(jnp.int32, shape, dim)


def nt_dot(a, b):
    return lax.dot_general(a, b, (((1,), (1,)), ((), ())), preferred_element_type=f32)


def layer_kernel(
    n_ctx,
    n_tensor,
    q_ref,
    k_ref,
    v_ref,
    ck_ref,
    cv_ref,
    res_ref,
    gain_ref,
    ids_ref,
    gw_ref,
    wg_hbm,
    wu_hbm,
    wd_hbm,
    o_ref,
    wg_buf,
    wu_buf,
    wd_buf,
    kv_own,
    kv_buf,
    hid,
    msg,
    got,
    xs,
    gate_sum,
    up_sum,
    act,
    back,
    landed,
    pick_main,
    pick_tail,
    gate_sem,
    up_sem,
    down_sem,
    kv_send,
    kv_recv,
    out_send,
    out_recv,
    pass_send,
    back_send,
    back_recv,
):
    c = lax.axis_index("ctx")
    z = lax.axis_index("tensor")
    me = c * n_tensor + z
    rows, quarter = res_ref.shape
    groups = quarter // LANES
    hidden = wd_hbm.shape[0]
    n_blocks = hidden // BLOCK
    per_expert = n_ctx * n_tensor // EXPERTS
    n_dev = n_ctx * n_tensor

    z_order = (
        (2, lax.rem(z + 2, 4)),
        (3, 3 - z),
        (1, z + 1 - 2 * lax.rem(z, 2)),
        (0, z),
    )

    pair = z // 2
    mate = z + 1 - 2 * lax.rem(z, 2)
    near = 2 - pair
    far = 3 - 3 * pair
    is_relay = z == 1 + pair
    end = 3 * pair
    k_order = (z, mate, near, far)

    def ctx_at(dc):
        return lax.rem(c + dc, n_ctx)

    barrier = pltpu.get_barrier_semaphore()
    for jz, zp in z_order:
        for dc in range(n_ctx):
            if jz or dc:
                pl.semaphore_signal(
                    barrier,
                    inc=1,
                    device_id={"ctx": ctx_at(dc), "tensor": zp},
                    device_id_type=MESH,
                )
    kv_own[0, 0] = ck_ref[...]
    kv_own[0, 1] = cv_ref[...]
    kv_own[1, 0] = k_ref[...]
    kv_own[1, 1] = v_ref[...]
    pl.semaphore_wait(barrier, n_dev - 1)

    kv_copies = []
    for dc in range(1, n_ctx):
        copy = pltpu.make_async_remote_copy(
            src_ref=kv_own.at[1 - (c + dc) // n_ctx],
            dst_ref=kv_buf.at[c],
            send_sem=kv_send.at[dc],
            recv_sem=kv_recv.at[c],
            device_id={"ctx": ctx_at(dc), "tensor": z},
            device_id_type=MESH,
        )
        copy.start()
        kv_copies.append(copy)

    def gate_copy(step):
        slot = step % GATE_SLOTS
        rows_in = pl.ds(pl.multiple_of(k_order[step] * quarter, quarter), quarter)
        return (
            pltpu.make_async_copy(wg_hbm.at[rows_in], wg_buf.at[slot], gate_sem.at[slot]),
            pltpu.make_async_copy(wu_hbm.at[rows_in], wu_buf.at[slot], up_sem.at[slot]),
        )

    def down_copy(step):
        zp = z_order[step][1]
        slot = step % DOWN_SLOTS
        cols = pl.ds(pl.multiple_of(zp * quarter, quarter), quarter)
        return pltpu.make_async_copy(wd_hbm.at[:, cols], wd_buf.at[slot], down_sem.at[slot])

    for step in range(GATE_SLOTS):
        for copy in gate_copy(step):
            copy.start()
    for step in range(DOWN_SLOTS):
        down_copy(step).start()

    ids = ids_ref[...]
    id_k = (ids[:, 0:1], ids[:, 1:2])
    lane = iota((rows, 128), 1)
    member = ((lane == id_k[0]) | (lane == id_k[1])).astype(f32).astype(bf16)
    earlier = (iota((rows, rows), 0) > iota((rows, rows), 1)).astype(f32).astype(bf16)
    count = jnp.dot(earlier, member, preferred_element_type=f32)
    rank_k = tuple(
        jnp.sum(jnp.where(lane == e, count, 0.0), axis=1, keepdims=True).astype(jnp.int32)
        for e in id_k
    )

    l_main = iota((rows, EXPERTS * MAIN), 1)
    s_main = jnp.zeros((rows, EXPERTS * MAIN), f32)
    l_tail = iota((rows, EXPERTS * TAIL), 1)
    s_tail = jnp.zeros((rows, EXPERTS * TAIL), f32)
    for k in range(TOP):
        s_main += (
            (id_k[k] == l_main // MAIN) & (rank_k[k] == l_main % MAIN)
        ).astype(f32)
        s_tail += (
            (id_k[k] == l_tail // TAIL) & (rank_k[k] == MAIN + l_tail % 4)
        ).astype(f32)
    s_main = s_main.T.astype(bf16)
    s_tails = [
        jnp.where(l_tail % TAIL // 4 == g, s_tail, 0.0).T.astype(bf16) for g in range(groups)
    ]
    p_main = iota((rows, n_dev * MAIN), 1)
    p_tail = iota((rows, n_dev * TAIL), 1)
    for k in range(TOP):
        pick_main[k] = (
            ((id_k[k] == p_main // (MAIN * per_expert)) & (rank_k[k] == p_main % MAIN))
            .astype(f32)
            .astype(bf16)
        )
        for g in range(groups):
            pick_tail[k, g] = (
                (
                    (id_k[k] == p_tail // (TAIL * per_expert))
                    & (rank_k[k] == MAIN + p_tail % 4)
                    & (p_tail % TAIL // 4 == g)
                )
                .astype(f32)
                .astype(bf16)
            )

    for dc in range(1, n_ctx):
        peer = ctx_at(dc)
        pltpu.make_async_remote_copy(
            src_ref=kv_own.at[0],
            dst_ref=kv_buf.at[peer],
            send_sem=kv_send.at[0],
            recv_sem=kv_recv.at[peer],
            device_id={"ctx": peer, "tensor": z},
            device_id_type=MESH,
        ).wait_recv()
    key_rest = jnp.concatenate([kv_buf[ctx_at(dc), 0] for dc in range(1, n_ctx)], axis=0)
    value_rest = jnp.concatenate([kv_buf[ctx_at(dc), 1] for dc in range(1, n_ctx)], axis=0)
    seen = iota((rows, rows), 1) <= iota((rows, rows), 0)
    scale = 1.0 / math.sqrt(HEAD_DIM)
    for h in range(quarter // HEAD_DIM):
        cols = slice(h * HEAD_DIM, (h + 1) * HEAD_DIM)
        head = q_ref[:, cols]
        s_rest = nt_dot(head, key_rest) * scale
        s_own = jnp.where(seen, nt_dot(head, k_ref[...]), nt_dot(head, ck_ref[...])) * scale
        top = jnp.maximum(
            jnp.max(s_rest, axis=1, keepdims=True), jnp.max(s_own, axis=1, keepdims=True)
        )
        w_rest = jnp.exp(s_rest - top)
        w_own = jnp.exp(s_own - top)
        total = jnp.sum(w_rest, axis=1, keepdims=True) + jnp.sum(w_own, axis=1, keepdims=True)
        summed = jnp.dot(w_rest.astype(bf16), value_rest, preferred_element_type=f32)
        summed += jnp.dot(
            jnp.where(seen, w_own, 0.0).astype(bf16), v_ref[...], preferred_element_type=f32
        )
        summed += jnp.dot(
            jnp.where(seen, 0.0, w_own).astype(bf16), cv_ref[...], preferred_element_type=f32
        )
        hid[:, cols] = (res_ref[:, cols].astype(f32) + summed / total).astype(bf16)

    tails = jnp.zeros((EXPERTS * TAIL, LANES), f32)
    for g in range(groups):
        part = hid[:, g * LANES : (g + 1) * LANES]
        chosen = jnp.dot(s_main, part, preferred_element_type=f32).astype(bf16)
        msg[:, g * MAIN : (g + 1) * MAIN, :] = chosen.reshape(EXPERTS, MAIN, LANES)
        tails += jnp.dot(s_tails[g], part, preferred_element_type=f32)
    msg[:, groups * MAIN :, :] = tails.astype(bf16).reshape(EXPERTS, TAIL, LANES)
    out_copies = []
    for t, zp in enumerate((near, mate, z)):
        for dc in range(n_ctx):
            cp = ctx_at(dc)
            to = (cp * n_tensor + zp) // per_expert
            if t < 2 or dc:
                copy = pltpu.make_async_remote_copy(
                    src_ref=msg.at[to],
                    dst_ref=got.at[c, z],
                    send_sem=out_send.at[t * n_ctx + dc],
                    recv_sem=out_recv.at[me],
                    device_id={"ctx": cp, "tensor": zp},
                    device_id_type=MESH,
                )
                copy.start()
                out_copies.append(copy)
            else:
                got[c, z] = msg[to]

    def arrival(cp, zq):
        pltpu.make_async_remote_copy(
            src_ref=msg.at[0],
            dst_ref=got.at[cp, zq],
            send_sem=out_send.at[0],
            recv_sem=out_recv.at[cp * n_tensor + zq],
            device_id={"ctx": ctx_at(1), "tensor": zq},
            device_id_type=MESH,
        ).wait_recv()

    def passing(t, zq, dc):
        cp = ctx_at(dc)
        return pltpu.make_async_remote_copy(
            src_ref=got.at[cp, zq],
            dst_ref=got.at[cp, zq],
            send_sem=pass_send.at[t * n_ctx + dc],
            recv_sem=out_recv.at[cp * n_tensor + zq],
            device_id={"ctx": c, "tensor": end},
            device_id_type=MESH,
        )

    fold_r = iota((n_ctx * 4, n_ctx * TAIL), 0)
    fold_c = iota((n_ctx * 4, n_ctx * TAIL), 1)
    fold = [
        (
            (fold_r // 4 == fold_c // TAIL)
            & (fold_r % 4 == fold_c % 4)
            & (fold_c % TAIL // 4 == g)
        )
        .astype(f32)
        .astype(bf16)
        for g in range(groups)
    ]
    items = xs.shape[0]
    squares = jnp.zeros((items, 1), f32)
    for step, zq in enumerate(k_order):
        if step < 2:
            for dc in range(n_ctx):
                if step or dc:
                    arrival(ctx_at(dc), zq)
        else:

            @pl.when(jnp.logical_not(is_relay))
            def _():
                for dc in range(n_ctx):
                    arrival(ctx_at(dc), zq)

        parts = [
            jnp.concatenate(
                [got[cp, zq, g * MAIN : (g + 1) * MAIN, :] for g in range(groups)], axis=1
            ).astype(f32)
            for cp in range(n_ctx)
        ]
        folded = got[:, zq, groups * MAIN :, :].reshape(n_ctx * TAIL, LANES)
        parts.append(
            jnp.concatenate(
                [jnp.dot(fold[g], folded, preferred_element_type=f32) for g in range(groups)],
                axis=1,
            )
        )
        wide = jnp.concatenate(parts, axis=0)
        squares += jnp.sum(wide * wide, axis=1, keepdims=True)
        gain = gain_ref[:, pl.ds(pl.multiple_of(zq * quarter, quarter), quarter)]
        xs[...] = (wide * gain).astype(bf16)
        for copy in gate_copy(step):
            copy.wait()
        slot = step % GATE_SLOTS
        last = step == n_tensor - 1
        if last:
            inverse = lax.rsqrt(squares / (quarter * n_tensor) + eps)

        def gate_block(b, carry):
            cols = pl.ds(pl.multiple_of(b * BLOCK, BLOCK), BLOCK)
            gate = jnp.dot(xs[...], wg_buf[slot, :, cols], preferred_element_type=f32)
            up = jnp.dot(xs[...], wu_buf[slot, :, cols], preferred_element_type=f32)
            if step:
                gate += gate_sum[:, cols]
                up += up_sum[:, cols]
            if last:
                gate *= inverse
                up *= inverse
                act[:, cols] = (gate / (1.0 + jnp.exp(-gate)) * up).astype(bf16)
            else:
                gate_sum[:, cols] = gate
                up_sum[:, cols] = up
            return carry

        lax.fori_loop(0, n_blocks, gate_block, 0)
        if step + GATE_SLOTS < n_tensor:
            for copy in gate_copy(step + GATE_SLOTS):
                copy.start()
        if step == 0:

            @pl.when(is_relay)
            def _():
                for t in (0, 1):
                    for dc in range(n_ctx):
                        arrival(ctx_at(dc), k_order[2 + t])
                        passing(t, k_order[2 + t], dc).start()

    fold_r = iota((n_ctx * TAIL, n_ctx * 4), 0)
    fold_c = iota((n_ctx * TAIL, n_ctx * 4), 1)
    back_copies = []
    for step, (jz, zp) in enumerate(z_order):
        down_copy(step).wait()
        part = jnp.dot(
            act[...], wd_buf[step % DOWN_SLOTS], preferred_element_type=f32
        ).astype(bf16)
        if step + DOWN_SLOTS < n_tensor:
            down_copy(step + DOWN_SLOTS).start()
        tails = jnp.zeros((n_ctx * TAIL, LANES), f32)
        for g in range(groups):
            cols = slice(g * LANES, (g + 1) * LANES)
            back[jz, :, g * MAIN : (g + 1) * MAIN, :] = part[: n_ctx * MAIN, cols].reshape(
                n_ctx, MAIN, LANES
            )
            unfold = (
                (
                    (fold_c // 4 == fold_r // TAIL)
                    & (fold_c % 4 == fold_r % 4)
                    & (fold_r % TAIL // 4 == g)
                )
                .astype(f32)
                .astype(bf16)
            )
            tails += jnp.dot(unfold, part[n_ctx * MAIN :, cols], preferred_element_type=f32)
        back[jz, :, groups * MAIN :, :] = tails.astype(bf16).reshape(n_ctx, TAIL, LANES)
        for dc in range(n_ctx):
            cp = ctx_at(dc)
            if jz or dc:
                copy = pltpu.make_async_remote_copy(
                    src_ref=back.at[jz, cp],
                    dst_ref=landed.at[me],
                    send_sem=back_send.at[jz * n_ctx + dc],
                    recv_sem=back_recv.at[me],
                    device_id={"ctx": cp, "tensor": zp},
                    device_id_type=MESH,
                )
                copy.start()
                back_copies.append(copy)
            else:
                landed[me] = back[jz, cp]
    for jz, zp in z_order[::-1]:
        for dc in range(n_ctx):
            if jz or dc:
                cp = ctx_at(dc)
                peer = cp * n_tensor + zp
                pltpu.make_async_remote_copy(
                    src_ref=back.at[0, 0],
                    dst_ref=landed.at[peer],
                    send_sem=back_send.at[0],
                    recv_sem=back_recv.at[peer],
                    device_id={"ctx": cp, "tensor": zp},
                    device_id_type=MESH,
                ).wait_recv()

    ends = landed[:, groups * MAIN :, :].reshape(n_dev * TAIL, LANES)
    for g in range(groups):
        cols = slice(g * LANES, (g + 1) * LANES)
        body = landed[:, g * MAIN : (g + 1) * MAIN, :].reshape(n_dev * MAIN, LANES)
        sums = hid[:, cols].astype(f32)
        for k in range(TOP):
            found = jnp.dot(pick_main[k], body, preferred_element_type=f32)
            found += jnp.dot(pick_tail[k, g], ends, preferred_element_type=f32)
            sums += gw_ref[:, k : k + 1] * found
        o_ref[:, cols] = sums.astype(bf16)
    for copy in kv_copies + out_copies + back_copies:
        copy.wait_send()

    @pl.when(is_relay)
    def _():
        for t in (0, 1):
            for dc in range(n_ctx):
                passing(t, k_order[2 + t], dc).wait_send()


def fused(
    queries,
    keys,
    values,
    cache_keys,
    cache_values,
    residual,
    norm_gain,
    w_gate,
    w_up,
    w_down,
    expert_ids,
    gate_weights,
):
    n_ctx = lax.axis_size("ctx")
    n_tensor = lax.axis_size("tensor")
    rows, quarter = residual.shape
    width = w_gate.shape[0]
    hidden = w_gate.shape[1]
    n_dev = n_ctx * n_tensor
    length = quarter // LANES * MAIN + TAIL
    items = n_ctx * CAP
    vmem = pl.BlockSpec(memory_space=pltpu.VMEM)
    hbm = pl.BlockSpec(memory_space=pl.ANY)
    dma = pltpu.SemaphoreType.DMA

    def kernel(*refs):
        layer_kernel(n_ctx, n_tensor, *refs)

    return pl.pallas_call(
        kernel,
        out_shape=jax.ShapeDtypeStruct(residual.shape, bf16),
        in_specs=[vmem] * 9 + [hbm] * 3,
        out_specs=vmem,
        scratch_shapes=[
            pltpu.VMEM((GATE_SLOTS, quarter, hidden), bf16),
            pltpu.VMEM((GATE_SLOTS, quarter, hidden), bf16),
            pltpu.VMEM((DOWN_SLOTS, hidden, quarter), bf16),
            pltpu.VMEM((2, 2, rows, HEAD_DIM), bf16),
            pltpu.VMEM((n_ctx, 2, rows, HEAD_DIM), bf16),
            pltpu.VMEM((rows, quarter), bf16),
            pltpu.VMEM((EXPERTS, length, LANES), bf16),
            pltpu.VMEM((n_ctx, n_tensor, length, LANES), bf16),
            pltpu.VMEM((items, quarter), bf16),
            pltpu.VMEM((items, hidden), f32),
            pltpu.VMEM((items, hidden), f32),
            pltpu.VMEM((items, hidden), bf16),
            pltpu.VMEM((n_tensor, n_ctx, length, LANES), bf16),
            pltpu.VMEM((n_dev, length, LANES), bf16),
            pltpu.VMEM((TOP, rows, n_dev * MAIN), bf16),
            pltpu.VMEM((TOP, quarter // LANES, rows, n_dev * TAIL), bf16),
            dma((GATE_SLOTS,)),
            dma((GATE_SLOTS,)),
            dma((DOWN_SLOTS,)),
            dma((n_ctx,)),
            dma((n_ctx,)),
            dma((n_dev,)),
            dma((n_dev,)),
            dma((2 * n_ctx,)),
            dma((n_dev,)),
            dma((n_dev,)),
        ],
        compiler_params=pltpu.CompilerParams(
            collective_id=0, has_side_effects=True, vmem_limit_bytes=63 * 1024 * 1024
        ),
        cost_estimate=pl.CostEstimate(
            flops=6 * items * width * hidden,
            bytes_accessed=6 * width * hidden,
            transcendentals=items * hidden,
        ),
    )(
        queries,
        keys,
        values,
        cache_keys,
        cache_values,
        residual,
        norm_gain.reshape(1, width),
        expert_ids,
        gate_weights,
        w_gate,
        w_up,
        w_down,
    )


def solution(mesh):
    in_specs = (
        P(("dp", "ctx"), "tensor"),
        P(("dp", "ctx"), "tensor"),
        P(("dp", "ctx"), "tensor"),
        P(("dp", "ctx"), "tensor"),
        P(("dp", "ctx"), "tensor"),
        P(("dp", "ctx"), "tensor"),
        P(),
        P(None, ("ctx", "tensor")),
        P(None, ("ctx", "tensor")),
        P(("ctx", "tensor"), None),
        P(("dp", "ctx"), None),
        P(("dp", "ctx"), None),
    )
    out_specs = P(("dp", "ctx"), "tensor")
    fits = mesh.shape["ctx"] == 4 and mesh.shape["tensor"] == 4
    return jax.shard_map(
        fused if fits else per_device, mesh=mesh, in_specs=in_specs, out_specs=out_specs, check_vma=False
    )
```
